128 devices in a mesh: row: 16 (over x, z_hi, core), col: 8 (over y, z_lo).
Axes of the slice: x: 4, y: 4, z: 4 (z_hi: 2, z_lo: 2; z = z_hi * 2 + z_lo), core: 2. Of those that a mesh axis runs over, the one named last changes fastest.
Arguments:
- inputs: bfloat16 [512, 8192], P('row', 'col'), may hold values from -6 to 6
- out_grad: bfloat16 [512, 8192], P('row', 'col'), may hold values from -6 to 6
- gate_weight: bfloat16 [8192, 28672], P('col', 'row'), may hold values from -0.0625 to 0.0625
- up_weight: bfloat16 [8192, 28672], P('col', 'row'), may hold values from -0.0625 to 0.0625
- down_weight: bfloat16 [28672, 8192], P('row', 'col'), may hold values from -0.03125 to 0.03125
Outputs:
- input_grad: bfloat16 [512, 8192], P('row', 'col')
- gate_weight_grad: bfloat16 [8192, 28672], P('col', 'row')
- up_weight_grad: bfloat16 [8192, 28672], P('col', 'row')
- down_weight_grad: bfloat16 [28672, 8192], P('row', 'col')
The draws below stay inside these ranges and needn't reach their ends.
All inputs are finite; a program needn't handle non-finite values.
Results may differ from the reference program's by a relative error of at most 0.005.
Values may be sent and summed in bfloat16 or wider, within the bound.
No kernel may reach another device: no remote copies, remote signals or barrier semaphores. Data moves between devices by JAX's collectives and lax.ppermute only.
A program may use at most 128 MiB of HBM per device.

```python
import jax
import jax.numpy as jnp
from jax import lax

D = 8192
FF = 28672
TOKENS = 512


def level_of(rng, dims, cuts, smallest, largest):
    loudness, own = 1.0, jax.random.fold_in(rng, 6)
    for position, blocks in cuts:
        draws = jnp.exp(jax.random.uniform(jax.random.fold_in(own, position), (blocks,), jnp.float32, smallest / len(cuts), largest / len(cuts)))
        loudness = loudness * jnp.repeat(draws, dims[position] // blocks).reshape([-1 if axis == position else 1 for axis in range(len(dims))])
    return loudness


def scatter_about(own_key, dims, scale, reach, pieces=(), kind=jnp.bfloat16):
    array = scale * jax.random.normal(own_key, dims, jnp.float32)
    if pieces:
        array = array * level_of(own_key, dims, pieces, -0.22, 0.18)
    return jnp.clip(array, -reach, reach).astype(kind)


def setup_inputs(seed: int = 0) -> dict:
    keys = jax.random.split(jax.random.key(seed), 6)
    inputs = scatter_about(keys[0], (TOKENS, D), 1.0, 6.0, ((0, 16), (1, 8)))
    out_grad = scatter_about(keys[1], (TOKENS, D), 1.0, 6.0, ((0, 16), (1, 8)))
    gate_weight = scatter_about(keys[2], (D, FF), D ** -0.5, 0.0625, ((0, 8), (1, 16)))
    up_weight = scatter_about(keys[3], (D, FF), D ** -0.5, 0.0625, ((0, 8), (1, 16)))
    down_weight = scatter_about(keys[4], (FF, D), FF ** -0.5, 0.03125, ((0, 16), (1, 8)))
    return dict(inputs=inputs, out_grad=out_grad, gate_weight=gate_weight, up_weight=up_weight, down_weight=down_weight)


def contract_first(left, right):
    return lax.dot_general(left, right, (((0,), (0,)), ((), ())), preferred_element_type=jnp.float32)


def contract_last(left, right):
    return lax.dot_general(left, right, (((1,), (1,)), ((), ())), preferred_element_type=jnp.float32)


def reference(inputs, out_grad, gate_weight, up_weight, down_weight):
    gate = jnp.dot(inputs, gate_weight, preferred_element_type=jnp.float32)
    up = jnp.dot(inputs, up_weight, preferred_element_type=jnp.float32)
    hidden_grad = contract_last(out_grad, down_weight)
    sig = jax.nn.sigmoid(gate)
    hidden = (gate * sig * up).astype(jnp.bfloat16)
    gate_grad = (hidden_grad * up * sig * (1.0 + gate * (1.0 - sig))).astype(jnp.bfloat16)
    up_grad = (hidden_grad * gate * sig).astype(jnp.bfloat16)
    down_weight_grad = contract_first(hidden, out_grad).astype(jnp.bfloat16)
    gate_weight_grad = contract_first(inputs, gate_grad).astype(jnp.bfloat16)
    up_weight_grad = contract_first(inputs, up_grad).astype(jnp.bfloat16)
    input_grad = (contract_last(gate_grad, gate_weight) + contract_last(up_grad, up_weight)).astype(jnp.bfloat16)
    return input_grad, gate_weight_grad, up_weight_grad, down_weight_grad
```

```python
import functools

import jax
import jax.numpy as jnp
from jax import lax
from jax.experimental import pallas as pl
from jax.experimental.pallas import tpu as pltpu
from jax.sharding import PartitionSpec as P

BF16, F32 = jnp.bfloat16, jnp.float32
TILE = 256
VMEM = 48 * 1024 * 1024

COL = {"a": 2, "b": 6, "c": 1}
BIT = {"a": 4, "b": 2, "c": 1}
CORE, ZHI, XA, XB, XAB = 1, 2, 4, 12, 8


def swap(value, axis, mask):
    size = lax.axis_size(axis)
    return lax.ppermute(value, axis, [(i, i ^ mask) for i in range(size)])


def block_order(mine, dims):
    names = [
        sum(BIT[d] * ((place >> (2 - k)) & 1) for k, d in enumerate(dims))
        for place in range(8)
    ]
    return jnp.asarray(names, jnp.int32) ^ mine


def gather_rows(value):
    pair = jnp.concatenate([value, swap(value, "row", ZHI)], 0)
    half = jnp.concatenate(
        [pair] + [swap(pair, "row", mask) for mask in (XA, XB, XAB)], 0
    )
    both = jnp.concatenate([half, swap(half, "row", CORE)], 0)
    return both.reshape(8, -1, value.shape[1])


def cost(m, k, n, extra=0):
    return pl.CostEstimate(
        flops=2 * m * k * n,
        bytes_accessed=2 * (m * k + k * n + m * n) + extra,
        transcendentals=0,
    )


def reorder(order_ref, blocks_ref, out_ref):
    rows = blocks_ref.shape[1]
    for place in range(8):
        out_ref[place * rows : (place + 1) * rows, :] = blocks_ref[order_ref[place]]


def part_kernel(w_dim, order_ref, x_ref, w_ref, send_ref, keep_ref, x_scr):
    @pl.when(pl.program_id(0) == 0)
    def _():
        reorder(order_ref, x_ref, x_scr)

    part = lax.dot_general(
        x_scr[...], w_ref[...], (((1,), (w_dim,)), ((), ())), preferred_element_type=F32
    )
    half = part.shape[0] // 2
    keep_ref[...] = part[:half]
    send_ref[...] = part[half:].astype(BF16)


def partial_products(blocks, weight, w_dim, order):
    _, rows, depth = blocks.shape
    width = weight.shape[1 - w_dim]
    w_spec = (
        pl.BlockSpec((depth, TILE), lambda i, _: (0, i))
        if w_dim == 0
        else pl.BlockSpec((TILE, depth), lambda i, _: (i, 0))
    )
    half = pl.BlockSpec((4 * rows, TILE), lambda i, _: (0, i))
    return pl.pallas_call(
        functools.partial(part_kernel, w_dim),
        out_shape=(
            jax.ShapeDtypeStruct((4 * rows, width), BF16),
            jax.ShapeDtypeStruct((4 * rows, width), F32),
        ),
        grid_spec=pltpu.PrefetchScalarGridSpec(
            num_scalar_prefetch=1,
            grid=(width // TILE,),
            in_specs=[pl.BlockSpec((8, rows, depth), lambda i, _: (0, 0, 0)), w_spec],
            out_specs=(half, half),
            scratch_shapes=[pltpu.VMEM((8 * rows, depth), BF16)],
        ),
        compiler_params=pltpu.CompilerParams(vmem_limit_bytes=VMEM),
        cost_estimate=cost(8 * rows, depth, width),
    )(order, blocks, weight)


def sum_of_parts(send, keep, dims):
    far = swap(send, "col", COL[dims[0]])
    n = far.shape[0] // 4
    total = keep[: 2 * n] + far[: 2 * n].astype(F32)
    send = (keep[2 * n :] + far[2 * n :].astype(F32)).astype(BF16)
    far = swap(send, "col", COL[dims[1]])
    send = (total[n:] + far[n:].astype(F32)).astype(BF16)
    total = total[:n] + far[:n].astype(F32)
    return total + swap(send, "col", COL[dims[2]]).astype(F32)


def gather_blocks(block, dims):
    for dim in dims[:2]:
        block = jnp.concatenate([block, swap(block, "col", COL[dim])], 0)
    return block, swap(block, "col", COL[dims[2]])


def wide_kernel(near_ref, far_ref, xt_ref, out_ref):
    half = near_ref.shape[0]
    out_ref[...] = (
        jnp.dot(xt_ref[:, :half], near_ref[...], preferred_element_type=F32)
        + jnp.dot(xt_ref[:, half:], far_ref[...], preferred_element_type=F32)
    ).astype(BF16)


def wide_grad(halves, xt):
    half, width = halves[0].shape
    depth = xt.shape[0]
    return pl.pallas_call(
        wide_kernel,
        out_shape=jax.ShapeDtypeStruct((depth, width), BF16),
        grid=(width // TILE,),
        in_specs=[
            pl.BlockSpec((half, TILE), lambda i: (0, i)),
            pl.BlockSpec((half, TILE), lambda i: (0, i)),
            pl.BlockSpec(xt.shape, lambda i: (0, 0)),
        ],
        out_specs=pl.BlockSpec((depth, TILE), lambda i: (0, i)),
        compiler_params=pltpu.CompilerParams(vmem_limit_bytes=VMEM),
        cost_estimate=cost(depth, 2 * half, width),
    )(*halves, xt)


def tall_kernel(order_ref, near_ref, far_ref, g_ref, out_ref, g_scr):
    @pl.when(pl.program_id(0) == 0)
    def _():
        reorder(order_ref, g_ref, g_scr)

    half = near_ref.shape[0]
    first = (((0,), (0,)), ((), ()))
    out_ref[...] = (
        lax.dot_general(near_ref[...], g_scr[:half], first, preferred_element_type=F32)
        + lax.dot_general(far_ref[...], g_scr[half:], first, preferred_element_type=F32)
    ).astype(BF16)


def tall_grad(halves, g_blocks, order):
    half, width = halves[0].shape
    depth = g_blocks.shape[2]
    return pl.pallas_call(
        tall_kernel,
        out_shape=jax.ShapeDtypeStruct((width, depth), BF16),
        grid_spec=pltpu.PrefetchScalarGridSpec(
            num_scalar_prefetch=1,
            grid=(width // TILE,),
            in_specs=[
                pl.BlockSpec((half, TILE), lambda i, _: (0, i)),
                pl.BlockSpec((half, TILE), lambda i, _: (0, i)),
                pl.BlockSpec(g_blocks.shape, lambda i, _: (0, 0, 0)),
            ],
            out_specs=pl.BlockSpec((TILE, depth), lambda i, _: (i, 0)),
            scratch_shapes=[pltpu.VMEM((2 * half, depth), BF16)],
        ),
        compiler_params=pltpu.CompilerParams(vmem_limit_bytes=VMEM),
        cost_estimate=cost(width, 2 * half, depth),
    )(order, *halves, g_blocks)


def input_kernel(
    gate_order, up_order, gn_ref, gf_ref, un_ref, uf_ref, wg_ref, wu_ref, keep_ref, send_ref, scr
):
    last = (((1,), (1,)), ((), ()))
    rows = scr.shape[1]

    def place(order, offset, rows_ref, w_ref, add):
        part = lax.dot_general(rows_ref[...], w_ref[...], last, preferred_element_type=F32)
        for k in range(4):
            piece = part[k * rows : (k + 1) * rows]
            where = order[offset + k]
            scr[where] = scr[where] + piece if add else piece

    place(gate_order, 0, gn_ref, wg_ref, False)
    place(gate_order, 4, gf_ref, wg_ref, False)
    place(up_order, 0, un_ref, wu_ref, True)
    place(up_order, 4, uf_ref, wu_ref, True)
    keep_ref[...] = scr[:4].reshape(keep_ref.shape)
    send_ref[...] = scr[4:].reshape(send_ref.shape)


def input_parts(gate_halves, gate_order, up_halves, up_order, gate_weight, up_weight):
    half, width = gate_halves[0].shape
    depth = gate_weight.shape[0]
    whole = pl.BlockSpec((half, width), lambda i, *_: (0, 0))
    w_spec = pl.BlockSpec((TILE, width), lambda i, *_: (i, 0))
    out = pl.BlockSpec((half, TILE), lambda i, *_: (0, i))
    shape = jax.ShapeDtypeStruct((half, depth), F32)
    return pl.pallas_call(
        input_kernel,
        out_shape=(shape, shape),
        grid_spec=pltpu.PrefetchScalarGridSpec(
            num_scalar_prefetch=2,
            grid=(depth // TILE,),
            in_specs=[whole] * 4 + [w_spec] * 2,
            out_specs=(out, out),
            scratch_shapes=[pltpu.VMEM((8, half // 4, TILE), F32)],
        ),
        compiler_params=pltpu.CompilerParams(vmem_limit_bytes=VMEM),
        cost_estimate=cost(2 * half, 2 * width, depth),
    )(gate_order, up_order, *gate_halves, *up_halves, gate_weight, up_weight)


def sum_rows(keep, send):
    total = keep + swap(send, "row", CORE)
    n = total.shape[0] // 4
    parts = [total[:n]]
    for k, mask in enumerate((XA, XB, XAB), 1):
        parts.append(swap(total[k * n : (k + 1) * n].astype(BF16), "row", mask).astype(F32))
    pair = (parts[0] + parts[1]) + (parts[2] + parts[3])
    return pair[: n // 2] + swap(pair[n // 2 :], "row", ZHI)


def swiglu_grads(gate, up, hidden_grad):
    sig = jax.nn.sigmoid(gate)
    hidden = (gate * sig * up).astype(BF16)
    gate_grad = (hidden_grad * up * sig * (1.0 + gate * (1.0 - sig))).astype(BF16)
    up_grad = (hidden_grad * gate * sig).astype(BF16)
    return hidden, gate_grad, up_grad


def ordered(blocks, order):
    return jnp.concatenate(
        [lax.dynamic_index_in_dim(blocks, order[s], 0, keepdims=False) for s in range(8)], 0
    )


def per_device(inputs, out_grad, gate_weight, up_weight, down_weight):
    col = lax.axis_index("col")
    y_high, y_low = (col >> 2) & 1, (col >> 1) & 1
    mine = (y_high ^ y_low) * BIT["a"] + y_high * BIT["b"] + (col & 1) * BIT["c"]
    mine = mine.astype(jnp.int32)

    x = gather_rows(inputs)
    g = gather_rows(out_grad)

    gate = sum_of_parts(*partial_products(x, gate_weight, 0, block_order(mine, "abc")), "abc")
    up = sum_of_parts(*partial_products(x, up_weight, 0, block_order(mine, "bca")), "bca")
    hidden_grad = sum_of_parts(
        *partial_products(g, down_weight, 1, block_order(mine, "cab")), "cab"
    )
    hidden, gate_grad, up_grad = swiglu_grads(gate, up, hidden_grad)

    gate_order = block_order(mine, "cba")
    up_order = block_order(mine, "acb")
    hidden_order = block_order(mine, "bac")
    gate_halves = gather_blocks(gate_grad, "abc")
    up_halves = gather_blocks(up_grad, "bca")
    hidden_halves = gather_blocks(hidden, "cab")

    keep, send = input_parts(
        gate_halves, gate_order, up_halves, up_order, gate_weight, up_weight
    )
    input_grad = sum_rows(keep, send).astype(BF16)
    gate_weight_grad = wide_grad(gate_halves, ordered(x, gate_order).T)
    up_weight_grad = wide_grad(up_halves, ordered(x, up_order).T)
    down_weight_grad = tall_grad(hidden_halves, g, hidden_order)
    return (input_grad, gate_weight_grad, up_weight_grad, down_weight_grad)


def solution(mesh):
    return jax.shard_map(
        per_device,
        mesh=mesh,
        in_specs=(
            P("row", "col"),
            P("row", "col"),
            P("col", "row"),
            P("col", "row"),
            P("row", "col"),
        ),
        out_specs=(P("row", "col"), P("col", "row"), P("col", "row"), P("row", "col")),
        check_vma=False,
    )
```

```python
import functools

import jax
import jax.numpy as jnp
from jax import lax
from jax.experimental import pallas as pl
from jax.experimental.pallas import tpu as pltpu
from jax.sharding import PartitionSpec as P

BF16, F32 = jnp.bfloat16, jnp.float32
TILE = 256
CHUNKS = 2
VMEM = 20 * 1024 * 1024

COL = {"a": 2, "b": 6, "c": 1}
BIT = {"a": 4, "b": 2, "c": 1}
CORE, ZHI, XA, XB, XAB = 1, 2, 4, 12, 8

SUM_DIMS = ("abc", "bca", "cab", "abc", "bca", "cab")
GATHER_DIMS = ("bca", "cab", "cab", "bca", "acb", "cba")


def swap(value, axis, mask):
    size = lax.axis_size(axis)
    return lax.ppermute(value, axis, [(i, i ^ mask) for i in range(size)])

IN_VMEM = pl.BlockSpec(memory_space=pltpu.VMEM)
IN_SMEM = pl.BlockSpec(memory_space=pltpu.SMEM)
PARAMS = pltpu.CompilerParams(vmem_limit_bytes=VMEM)


SHORT = pl.CostEstimate(flops=1, bytes_accessed=1, transcendentals=0)


def block_at(place, mine, dims):
    name = sum(BIT[d] * ((place >> (2 - k)) & 1) for k, d in enumerate(dims))
    return name ^ mine


def place_of(block, mine, dims):
    bits = [(((block ^ mine) // BIT[d]) % 2) * (4 >> k) for k, d in enumerate(dims)]
    return bits[0] + bits[1] + bits[2]


class Order:
    def __init__(self, mine):
        self.mine = mine

    def run(self, call, *args):
        out = call(self.mine, *args)
        self.mine, out = lax.optimization_barrier((self.mine, out))
        return out


def small(kernel, shapes, count):
    return pl.pallas_call(
        lambda mine, *refs: kernel(*refs),
        out_shape=shapes,
        in_specs=[IN_SMEM] + [IN_VMEM] * count,
        out_specs=[IN_VMEM] * len(shapes),
        compiler_params=PARAMS,
        cost_estimate=SHORT,
    )


def join_kernel(plan, *refs):
    ins, outs = refs[: -len(plan)], refs[-len(plan) :]
    for out, pieces in zip(outs, plan):
        at = 0
        for which, start, size in pieces:
            out[at : at + size, :] = ins[which][start : start + size, :]
            at += size


def join(order, arrays, *plan):
    width = arrays[0].shape[1]
    shapes = [
        jax.ShapeDtypeStruct((sum(p[2] for p in pieces), width), arrays[0].dtype)
        for pieces in plan
    ]
    out = order.run(
        small(functools.partial(join_kernel, plan), shapes, len(arrays)), *arrays
    )
    return out if len(out) > 1 else out[0]


def fetch_kernel(mine_ref, w_ref, out_ref, sem):
    copy = pltpu.make_async_copy(w_ref, out_ref, sem)
    copy.start()
    copy.wait()


def fetch(order, weight):
    return order.run(
        pl.pallas_call(
            fetch_kernel,
            out_shape=jax.ShapeDtypeStruct(weight.shape, weight.dtype),
            in_specs=[IN_SMEM, pl.BlockSpec(memory_space=pltpu.HBM)],
            out_specs=IN_VMEM,
            scratch_shapes=[pltpu.SemaphoreType.DMA],
            compiler_params=PARAMS,
            cost_estimate=SHORT,
        ),
        weight,
    )


def stack_kernel(a_ref, b_ref, out_ref, sems):
    n = a_ref.shape[0]
    copies = [
        pltpu.make_async_copy(ref, out_ref.at[k * n : (k + 1) * n], sems.at[k])
        for k, ref in enumerate((a_ref, b_ref))
    ]
    for copy in copies:
        copy.start()
    for copy in copies:
        copy.wait()


def stack(a, b):
    return pl.pallas_call(
        stack_kernel,
        out_shape=jax.ShapeDtypeStruct((2 * a.shape[0], a.shape[1]), a.dtype),
        in_specs=[pl.BlockSpec(memory_space=pltpu.HBM)] * 2,
        out_specs=IN_VMEM,
        scratch_shapes=[pltpu.SemaphoreType.DMA((2,))],
        compiler_params=PARAMS,
        cost_estimate=SHORT,
    )(a, b)


def part_kernel(w_dim, dims, first, cols, mine_ref, x_ref, w_ref, out_ref, x_scr):
    rows = x_ref.shape[1]
    for k in range(4):
        x_scr[k * rows : (k + 1) * rows, :] = x_ref[block_at(first + k, mine_ref[0], dims)]
    w = w_ref[:, cols] if w_dim == 0 else w_ref[cols, :]
    out_ref[...] = lax.dot_general(
        x_scr[...], w, (((1,), (w_dim,)), ((), ())), preferred_element_type=F32
    ).astype(out_ref.dtype)


def partial_product(order, blocks, weight, w_dim, dims, first, cols, dtype):
    _, rows, depth = blocks.shape
    width = cols.stop - cols.start
    call = pl.pallas_call(
        functools.partial(part_kernel, w_dim, dims, first, cols),
        out_shape=jax.ShapeDtypeStruct((4 * rows, width), dtype),
        in_specs=[IN_SMEM, IN_VMEM, IN_VMEM],
        out_specs=IN_VMEM,
        scratch_shapes=[pltpu.VMEM((4 * rows, depth), BF16)],
        compiler_params=PARAMS,
        cost_estimate=SHORT,
    )
    return order.run(call, blocks, weight)


def halve_kernel(keep_ref, far_ref, send_ref, total_ref):
    n = send_ref.shape[0]
    send_ref[...] = (keep_ref[n:, :] + far_ref[n:, :].astype(F32)).astype(BF16)
    total_ref[...] = keep_ref[:n, :] + far_ref[:n, :].astype(F32)


def halve(order, keep, far):
    shape = (far.shape[0] // 2, far.shape[1])
    shapes = [jax.ShapeDtypeStruct(shape, BF16), jax.ShapeDtypeStruct(shape, F32)]
    return order.run(small(halve_kernel, shapes, 2), keep, far)


def swiglu_kernel(*refs):
    gate, up, hidden_grad = (
        refs[2 * k][...] + refs[2 * k + 1][...].astype(F32) for k in range(3)
    )
    for ref, value in zip(refs[6:], swiglu_grads(gate, up, hidden_grad)):
        ref[...] = value


def swiglu(order, totals, fars):
    shape = jax.ShapeDtypeStruct(totals[0].shape, BF16)
    args = [a for pair in zip(totals, fars) for a in pair]
    return order.run(small(swiglu_kernel, [shape] * 3, 6), *args)


def reorder(dims, mine_ref, blocks_ref, out_ref):
    rows = blocks_ref.shape[1]
    for place in range(8):
        out_ref[place * rows : (place + 1) * rows, :] = blocks_ref[
            block_at(place, mine_ref[0], dims)
        ]


FIRST = (((0,), (0,)), ((), ()))
LAST = (((1,), (1,)), ((), ()))


def grad_pieces(out_ref, out_scr, sems, rows_at, cols, pieces):
    copies = []
    for k, (rows, value) in enumerate(pieces):
        out_scr[rows, :] = value().astype(BF16)
        there = slice(rows_at + rows.start, rows_at + rows.stop)
        copies.append(
            pltpu.make_async_copy(out_scr.at[rows], out_ref.at[there, cols], sems.at[k])
        )
        copies[-1].start()
    for copy in copies:
        copy.wait()


def wide_kernel(dims, cols, mine_ref, x_ref, grad_ref, *rest):
    out_ref, x_scr, out_scr, sems = rest[-4:]
    reorder(dims, mine_ref, x_ref, x_scr)
    half = out_scr.shape[0] // 2

    def product(rows):
        return lambda: lax.dot_general(
            x_scr[:, rows], grad_ref[...], FIRST, preferred_element_type=F32
        )

    parts = (slice(0, half), slice(half, 2 * half))
    grad_pieces(out_ref, out_scr, sems, 0, cols, [(rows, product(rows)) for rows in parts])


def tall_kernel(dims, at, mine_ref, g_ref, hidden_ref, *rest):
    out_ref, g_scr, out_scr, sems = rest[-4:]
    reorder(dims, mine_ref, g_ref, g_scr)
    width = out_scr.shape[0]
    half = -(-width // 256) * 128

    def product(rows):
        return lambda: lax.dot_general(
            hidden_ref[:, rows], g_scr[...], FIRST, preferred_element_type=F32
        )

    parts = (slice(0, half), slice(half, width))
    grad_pieces(
        out_ref, out_scr, sems, at, slice(None), [(rows, product(rows)) for rows in parts]
    )


def weight_grad(order, kernel, shape, piece, blocks, grad, before):
    _, rows, depth = blocks.shape
    tokens, width = grad.shape
    more = [] if before is None else [before]
    call = pl.pallas_call(
        kernel,
        out_shape=jax.ShapeDtypeStruct(shape, BF16),
        in_specs=[IN_SMEM, IN_VMEM, IN_VMEM] + [pl.BlockSpec(memory_space=pltpu.HBM)] * len(more),
        out_specs=pl.BlockSpec(memory_space=pl.ANY),
        scratch_shapes=[
            pltpu.VMEM((tokens, depth), BF16),
            pltpu.VMEM(piece, BF16),
            pltpu.SemaphoreType.DMA((2,)),
        ],
        input_output_aliases={3: 0} if more else {},
        compiler_params=PARAMS,
        cost_estimate=SHORT,
    )
    return order.run(call, blocks, grad, *more)


def input_kernel(first, gate_dims, up_dims, cols, mine_ref, gg_ref, ug_ref, wg_ref, wu_ref, *rest):
    out_ref, gg_scr, ug_scr = rest[-3:]
    mine = mine_ref[0]
    rows = gg_ref.shape[1]
    for k in range(4):
        here = slice(k * rows, (k + 1) * rows)
        gg_scr[here, :] = gg_ref[place_of(first + k, mine, gate_dims)]
        ug_scr[here, :] = ug_ref[place_of(first + k, mine, up_dims)]
    for i in range(0, out_ref.shape[1], TILE):
        here = slice(i, i + TILE)
        part = lax.dot_general(
            gg_scr[...], wg_ref[here, cols], LAST, preferred_element_type=F32
        ) + lax.dot_general(ug_scr[...], wu_ref[here, cols], LAST, preferred_element_type=F32)
        out_ref[:, here] = part + rest[0][:, here] if len(rest) == 4 else part


def input_part(order, first, grads, dims, weights, cols, before):
    tokens, width = grads[0].shape
    depth = weights[0].shape[0]
    half = pltpu.VMEM((tokens // 2, width), BF16)
    blocked = (8, tokens // 8, width)
    more = [] if before is None else [before]
    call = pl.pallas_call(
        functools.partial(input_kernel, first, *dims, cols),
        out_shape=jax.ShapeDtypeStruct((tokens // 2, depth), F32),
        in_specs=[IN_SMEM] + [IN_VMEM] * (4 + len(more)),
        out_specs=IN_VMEM,
        scratch_shapes=[half, half],
        compiler_params=PARAMS,
        cost_estimate=SHORT,
    )
    return order.run(call, *(v.reshape(blocked) for v in grads), *weights, *more)


def core_kernel(keep_ref, far_ref, own_ref, *send_refs):
    n = own_ref.shape[0]
    own_ref[...] = keep_ref[:n, :] + far_ref[:n, :]
    for k, ref in enumerate(send_refs, 1):
        here = slice(k * n, (k + 1) * n)
        ref[...] = (keep_ref[here, :] + far_ref[here, :]).astype(BF16)


def ring_kernel(own_ref, a_ref, b_ref, c_ref, keep_ref, send_ref):
    total = (own_ref[...] + a_ref[...].astype(F32)) + (
        b_ref[...].astype(F32) + c_ref[...].astype(F32)
    )
    n = keep_ref.shape[0]
    keep_ref[...] = total[:n]
    send_ref[...] = total[n:]


def swiglu_grads(gate, up, hidden_grad):
    sig = jax.nn.sigmoid(gate)
    hidden = (gate * sig * up).astype(BF16)
    gate_grad = (hidden_grad * up * sig * (1.0 + gate * (1.0 - sig))).astype(BF16)
    up_grad = (hidden_grad * gate * sig).astype(BF16)
    return hidden, gate_grad, up_grad


def per_device(inputs, out_grad, gate_weight, up_weight, down_weight):
    col = lax.axis_index("col")
    y_high, y_low = (col >> 2) & 1, (col >> 1) & 1
    mine = (y_high ^ y_low) * BIT["a"] + y_high * BIT["b"] + (col & 1) * BIT["c"]
    mine = mine.astype(jnp.int32).reshape(1)

    order = Order(mine)
    depth, width = gate_weight.shape
    size = width // CHUNKS
    chunks = [slice(k * size, (k + 1) * size) for k in range(CHUNKS)]
    n = inputs.shape[0]
    own = stack(inputs, out_grad)
    far = swap(own, "row", ZHI)
    weights = [fetch(order, gate_weight)]
    x, g = join(order, (own, far), ((0, 0, n), (1, 0, n)), ((0, n, n), (1, n, n)))
    far_x, far_g = swap(x, "row", XA), swap(g, "row", XB)
    weights.append(fetch(order, up_weight))
    n = 2 * n
    x, g = join(order, (x, far_x, g, far_g), ((0, 0, n), (1, 0, n)), ((2, 0, n), (3, 0, n)))
    far_x, far_g = swap(x, "row", XB), swap(g, "row", XA)
    weights.append(fetch(order, down_weight))
    x, g = join(
        order,
        (x, far_x, g, far_g),
        ((0, 0, 2 * n), (1, 0, 2 * n)),
        ((2, 0, n), (3, 0, n), (2, n, n), (3, n, n)),
    )
    far_x, far_g = swap(x, "row", CORE), swap(g, "row", CORE)
    x = join(order, (x, far_x), ((0, 0, 4 * n), (1, 0, 4 * n))).reshape(8, n, -1)

    w_dims = (0, 0, 1)
    items = [(c, k) for c in range(CHUNKS) for k in range(3)]
    totals, fars = [None] * len(items), [None] * len(items)
    lefts = [x, x, None]

    def part(i, first, dtype):
        c, k = items[i]
        return partial_product(
            order, lefts[k], weights[k], w_dims[k], SUM_DIMS[i], first, chunks[c], dtype
        )

    for i, (_, k) in enumerate(items):
        if lefts[k] is None:
            lefts[k] = join(order, (g, far_g), ((0, 0, 4 * n), (1, 0, 4 * n))).reshape(x.shape)
        fars[i] = swap(part(i, 4, BF16), "col", COL[SUM_DIMS[i][0]])
    for step in (1, 2):
        for i, dims in enumerate(SUM_DIMS):
            if step == 1:
                totals[i] = part(i, 0, F32)
            send, totals[i] = halve(order, totals[i], fars[i])
            fars[i] = swap(send, "col", COL[dims[step]])

    grads = [None] * len(items)
    for c in range(CHUNKS):
        these = slice(3 * c, 3 * c + 3)
        hidden, gate_grad, up_grad = swiglu(order, totals[these], fars[these])
        grads[these] = gate_grad, up_grad, hidden
        for i in (3 * c, 3 * c + 1):
            fars[i] = swap(grads[i], "col", COL[GATHER_DIMS[i][0]])

    def grow(i, step):
        if step:
            n = fars[i].shape[0]
            grads[i] = join(order, (grads[i], fars[i]), ((0, 0, n), (1, 0, n)))
        if step < 3:
            fars[i] = swap(grads[i], "col", COL[GATHER_DIMS[i][step]])

    out = [None] * 3
    shapes = (((depth, width), (depth, size)),) * 2 + (((width, depth), (size, depth)),)

    def weight_step(i):
        c, k = items[i]
        place = GATHER_DIMS[i][::-1]
        kernel = (
            functools.partial(wide_kernel, place, chunks[c])
            if k < 2
            else functools.partial(tall_kernel, place, chunks[c].start)
        )
        out[k] = weight_grad(order, kernel, *shapes[k], lefts[k], grads[i], out[k])

    def input_step(c, first, before):
        these = slice(3 * c, 3 * c + 2)
        places = [dims[::-1] for dims in GATHER_DIMS[these]]
        return input_part(order, first, grads[these], places, weights[:2], chunks[c], before)

    for step in (1, 2):
        for i in (0, 1, 3, 4):
            grow(i, step)
    grow(2, 0)
    grow(5, 0)
    grow(0, 3)
    grow(1, 3)
    send, keep = input_step(0, 4, None), input_step(0, 0, None)
    grow(2, 1)
    grow(5, 1)
    weight_step(0)
    weight_step(1)
    grow(3, 3)
    grow(4, 3)
    send = input_step(1, 4, send)
    far = swap(send, "row", CORE)
    keep = input_step(1, 0, keep)

    n = x.shape[1]
    shape = (n, depth)
    own, *sends = order.run(
        small(
            core_kernel,
            [jax.ShapeDtypeStruct(shape, F32)] + [jax.ShapeDtypeStruct(shape, BF16)] * 3,
            2,
        ),
        keep,
        far,
    )
    rings = [swap(v, "row", mask) for v, mask in zip(sends, (XA, XB, XAB))]
    grow(2, 2)
    grow(5, 2)
    weight_step(3)
    shape = jax.ShapeDtypeStruct((n // 2, depth), F32)
    keep, send = order.run(small(ring_kernel, [shape, shape], 4), own, *rings)
    far = swap(send, "row", ZHI)
    weight_step(4)
    for i in (2, 5):
        grow(i, 3)
        weight_step(i)
    input_grad = (keep + far).astype(BF16)
    return (input_grad, *out)


def solution(mesh):
    return jax.shard_map(
        per_device,
        mesh=mesh,
        in_specs=(
            P("row", "col"),
            P("row", "col"),
            P("col", "row"),
            P("col", "row"),
            P("row", "col"),
        ),
        out_specs=(P("row", "col"), P("col", "row"), P("col", "row"), P("row", "col")),
        check_vma=False,
    )
```

```python
import functools

import jax
import jax.numpy as jnp
from jax import lax
from jax.experimental import pallas as pl
from jax.experimental.pallas import tpu as pltpu
from jax.sharding import PartitionSpec as P

BF16, F32 = jnp.bfloat16, jnp.float32
TILE = 256
CHUNKS = 2
VMEM = 20 * 1024 * 1024

COL = {"a": 2, "b": 6, "c": 1}
BIT = {"a": 4, "b": 2, "c": 1}
CORE, ZHI, XA, XB, XAB = 1, 2, 4, 12, 8

SUM_DIMS = ("abc", "bca", "cab", "abc", "bca", "cab")
GATHER_DIMS = ("bca", "cab", "cab", "bca", "acb", "cba")


def swap(value, axis, mask):
    size = lax.axis_size(axis)
    return lax.ppermute(value, axis, [(i, i ^ mask) for i in range(size)])

IN_VMEM = pl.BlockSpec(memory_space=pltpu.VMEM)
IN_SMEM = pl.BlockSpec(memory_space=pltpu.SMEM)
PARAMS = pltpu.CompilerParams(vmem_limit_bytes=VMEM)


SHORT = pl.CostEstimate(flops=1, bytes_accessed=1, transcendentals=0)


def block_at(place, mine, dims):
    name = sum(BIT[d] * ((place >> (2 - k)) & 1) for k, d in enumerate(dims))
    return name ^ mine


def place_of(block, mine, dims):
    bits = [(((block ^ mine) // BIT[d]) % 2) * (4 >> k) for k, d in enumerate(dims)]
    return bits[0] + bits[1] + bits[2]


class Order:
    def __init__(self, mine):
        self.mine = mine

    def run(self, call, *args):
        out = call(self.mine, *args)
        self.mine, out = lax.optimization_barrier((self.mine, out))
        return out


def small(kernel, shapes, count):
    return pl.pallas_call(
        lambda mine, *refs: kernel(*refs),
        out_shape=shapes,
        in_specs=[IN_SMEM] + [IN_VMEM] * count,
        out_specs=[IN_VMEM] * len(shapes),
        compiler_params=PARAMS,
        cost_estimate=SHORT,
    )


def join_kernel(plan, *refs):
    ins, outs = refs[: -len(plan)], refs[-len(plan) :]
    for out, pieces in zip(outs, plan):
        at = 0
        for which, start, size in pieces:
            out[at : at + size, :] = ins[which][start : start + size, :]
            at += size


def join(order, arrays, *plan):
    width = arrays[0].shape[1]
    shapes = [
        jax.ShapeDtypeStruct((sum(p[2] for p in pieces), width), arrays[0].dtype)
        for pieces in plan
    ]
    out = order.run(
        small(functools.partial(join_kernel, plan), shapes, len(arrays)), *arrays
    )
    return out if len(out) > 1 else out[0]


def fetch_kernel(mine_ref, w_ref, out_ref, sem):
    copy = pltpu.make_async_copy(w_ref, out_ref, sem)
    copy.start()
    copy.wait()


def fetch(order, weight):
    return order.run(
        pl.pallas_call(
            fetch_kernel,
            out_shape=jax.ShapeDtypeStruct(weight.shape, weight.dtype),
            in_specs=[IN_SMEM, pl.BlockSpec(memory_space=pltpu.HBM)],
            out_specs=IN_VMEM,
            scratch_shapes=[pltpu.SemaphoreType.DMA],
            compiler_params=PARAMS,
            cost_estimate=SHORT,
        ),
        weight,
    )


def part_kernel(w_dim, dims, first, cols, mine_ref, x_ref, w_ref, out_ref, x_scr):
    rows = x_ref.shape[1]
    for k in range(4):
        x_scr[k * rows : (k + 1) * rows, :] = x_ref[block_at(first + k, mine_ref[0], dims)]
    w = w_ref[:, cols] if w_dim == 0 else w_ref[cols, :]
    out_ref[...] = lax.dot_general(
        x_scr[...], w, (((1,), (w_dim,)), ((), ())), preferred_element_type=F32
    ).astype(out_ref.dtype)


def partial_product(order, blocks, weight, w_dim, dims, first, cols, dtype):
    _, rows, depth = blocks.shape
    width = cols.stop - cols.start
    call = pl.pallas_call(
        functools.partial(part_kernel, w_dim, dims, first, cols),
        out_shape=jax.ShapeDtypeStruct((4 * rows, width), dtype),
        in_specs=[IN_SMEM, IN_VMEM, IN_VMEM],
        out_specs=IN_VMEM,
        scratch_shapes=[pltpu.VMEM((4 * rows, depth), BF16)],
        compiler_params=PARAMS,
        cost_estimate=SHORT,
    )
    return order.run(call, blocks, weight)


def halve_kernel(keep_ref, far_ref, send_ref, total_ref):
    n = send_ref.shape[0]
    send_ref[...] = (keep_ref[n:, :] + far_ref[n:, :].astype(F32)).astype(BF16)
    total_ref[...] = keep_ref[:n, :] + far_ref[:n, :].astype(F32)


def halve(order, keep, far):
    shape = (far.shape[0] // 2, far.shape[1])
    shapes = [jax.ShapeDtypeStruct(shape, BF16), jax.ShapeDtypeStruct(shape, F32)]
    return order.run(small(halve_kernel, shapes, 2), keep, far)


def swiglu_kernel(*refs):
    gate, up, hidden_grad = (
        refs[2 * k][...] + refs[2 * k + 1][...].astype(F32) for k in range(3)
    )
    for ref, value in zip(refs[6:], swiglu_grads(gate, up, hidden_grad)):
        ref[...] = value


def swiglu(order, totals, fars):
    shape = jax.ShapeDtypeStruct(totals[0].shape, BF16)
    args = [a for pair in zip(totals, fars) for a in pair]
    return order.run(small(swiglu_kernel, [shape] * 3, 6), *args)


def beside_kernel(a_ref, b_ref, out_ref):
    width = a_ref.shape[1]
    out_ref[:, :width] = a_ref[...]
    out_ref[:, width:] = b_ref[...]


def beside(order, a, b):
    shape = jax.ShapeDtypeStruct((a.shape[0], a.shape[1] + b.shape[1]), a.dtype)
    return order.run(small(beside_kernel, [shape], 2), a, b)[0]


def split_kernel(near_ref, far_ref, *out_refs):
    rows, width = near_ref.shape[0], out_refs[0].shape[1]
    for k, ref in enumerate(out_refs):
        here = slice(k * width, (k + 1) * width)
        ref[:rows, :] = near_ref[:, here]
        ref[rows:, :] = far_ref[:, here]


def split(order, near, far, count):
    shape = jax.ShapeDtypeStruct((2 * near.shape[0], near.shape[1] // count), near.dtype)
    return order.run(small(split_kernel, [shape] * count, 2), near, far)


def reorder(dims, mine_ref, blocks_ref, out_ref):
    rows = blocks_ref.shape[1]
    for place in range(8):
        out_ref[place * rows : (place + 1) * rows, :] = blocks_ref[
            block_at(place, mine_ref[0], dims)
        ]


FIRST = (((0,), (0,)), ((), ()))
LAST = (((1,), (1,)), ((), ()))


def grads_kernel(jobs, mine_ref, *refs):
    count = len(jobs)
    lefts, grads = refs[:count], refs[count : 2 * count]
    kinds = sorted({kind for kind, _, _ in jobs})
    out_refs, (scrs, out_scrs, sems) = refs[-len(kinds) - 3 : -3], refs[-3:]
    copies = []
    for k, (kind, dims, cols) in enumerate(jobs):
        left_scr, out_scr, out_ref = scrs[k], out_scrs[k], out_refs[kinds.index(kind)]
        reorder(dims, mine_ref, lefts[k], left_scr)
        size = out_scr.shape[0]
        half = -(-size // 256) * 128
        for rows in (slice(0, half), slice(half, size)):
            if kind < 2:
                a, b = left_scr[:, rows], grads[k][...]
                there = out_ref.at[rows, cols]
            else:
                a, b = grads[k][:, rows], left_scr[...]
                there = out_ref.at[cols.start + rows.start : cols.start + rows.stop]
            out_scr[rows, :] = lax.dot_general(
                a, b, FIRST, preferred_element_type=F32
            ).astype(BF16)
            copies.append(pltpu.make_async_copy(out_scr.at[rows], there, sems.at[len(copies)]))
            copies[-1].start()
    for copy in copies:
        copy.wait()


def weight_grads(order, jobs, lefts, grads, shapes, befores):
    kinds = sorted({kind for kind, _, _ in jobs})
    in_hbm = pl.BlockSpec(memory_space=pltpu.HBM)
    known = [(at, befores[k]) for at, k in enumerate(kinds) if befores[k] is not None]
    sizes = [
        (shapes[kind][0], cols.stop - cols.start)
        if kind < 2
        else (cols.stop - cols.start, shapes[kind][1])
        for kind, _, cols in jobs
    ]
    flat = [(v.shape[0] * v.shape[1], v.shape[2]) for v in lefts]
    first = 1 + 2 * len(jobs)
    call = pl.pallas_call(
        functools.partial(grads_kernel, jobs),
        out_shape=[jax.ShapeDtypeStruct(shapes[k], BF16) for k in kinds],
        in_specs=[IN_SMEM] + [IN_VMEM] * (2 * len(jobs)) + [in_hbm] * len(known),
        out_specs=[pl.BlockSpec(memory_space=pl.ANY)] * len(kinds),
        scratch_shapes=[
            [pltpu.VMEM(shape, BF16) for shape in flat],
            [pltpu.VMEM(size, BF16) for size in sizes],
            pltpu.SemaphoreType.DMA((2 * len(jobs),)),
        ],
        input_output_aliases={first + at: k for at, (k, _) in enumerate(known)},
        compiler_params=PARAMS,
        cost_estimate=SHORT,
    )
    return order.run(call, *lefts, *grads, *(b for _, b in known))


def input_kernel(first, gate_dims, up_dims, cols, mine_ref, gg_ref, ug_ref, wg_ref, wu_ref, *rest):
    out_ref, gg_scr, ug_scr = rest[-3:]
    mine = mine_ref[0]
    rows = gg_ref.shape[1]
    for k in range(4):
        here = slice(k * rows, (k + 1) * rows)
        gg_scr[here, :] = gg_ref[place_of(first + k, mine, gate_dims)]
        ug_scr[here, :] = ug_ref[place_of(first + k, mine, up_dims)]
    for i in range(0, out_ref.shape[1], TILE):
        here = slice(i, i + TILE)
        part = lax.dot_general(
            gg_scr[...], wg_ref[here, cols], LAST, preferred_element_type=F32
        ) + lax.dot_general(ug_scr[...], wu_ref[here, cols], LAST, preferred_element_type=F32)
        out_ref[:, here] = part + rest[0][:, here] if len(rest) == 4 else part


def input_part(order, first, grads, dims, weights, cols, before):
    tokens, width = grads[0].shape
    depth = weights[0].shape[0]
    half = pltpu.VMEM((tokens // 2, width), BF16)
    blocked = (8, tokens // 8, width)
    more = [] if before is None else [before]
    call = pl.pallas_call(
        functools.partial(input_kernel, first, *dims, cols),
        out_shape=jax.ShapeDtypeStruct((tokens // 2, depth), F32),
        in_specs=[IN_SMEM] + [IN_VMEM] * (4 + len(more)),
        out_specs=IN_VMEM,
        scratch_shapes=[half, half],
        compiler_params=PARAMS,
        cost_estimate=SHORT,
    )
    return order.run(call, *(v.reshape(blocked) for v in grads), *weights, *more)


def core_kernel(keep_ref, far_ref, own_ref, *send_refs):
    n = own_ref.shape[0]
    own_ref[...] = keep_ref[:n, :] + far_ref[:n, :]
    for k, ref in enumerate(send_refs, 1):
        here = slice(k * n, (k + 1) * n)
        ref[...] = (keep_ref[here, :] + far_ref[here, :]).astype(BF16)


def ring_kernel(own_ref, a_ref, b_ref, c_ref, keep_ref, send_ref):
    total = (own_ref[...] + a_ref[...].astype(F32)) + (
        b_ref[...].astype(F32) + c_ref[...].astype(F32)
    )
    n = keep_ref.shape[0]
    keep_ref[...] = total[:n]
    send_ref[...] = total[n:]


def swiglu_grads(gate, up, hidden_grad):
    sig = jax.nn.sigmoid(gate)
    hidden = (gate * sig * up).astype(BF16)
    gate_grad = (hidden_grad * up * sig * (1.0 + gate * (1.0 - sig))).astype(BF16)
    up_grad = (hidden_grad * gate * sig).astype(BF16)
    return hidden, gate_grad, up_grad


def per_device(inputs, out_grad, gate_weight, up_weight, down_weight):
    col = lax.axis_index("col")
    y_high, y_low = (col >> 2) & 1, (col >> 1) & 1
    mine = (y_high ^ y_low) * BIT["a"] + y_high * BIT["b"] + (col & 1) * BIT["c"]
    mine = mine.astype(jnp.int32).reshape(1)

    order = Order(mine)
    depth, width = gate_weight.shape
    size = width // CHUNKS
    chunks = [slice(k * size, (k + 1) * size) for k in range(CHUNKS)]
    n = inputs.shape[0]
    far_x, far_g = swap(inputs, "row", ZHI), swap(out_grad, "row", ZHI)
    weights = [fetch(order, gate_weight)]
    both = join(order, (inputs, far_x, out_grad, far_g), tuple((k, 0, n) for k in range(4)))
    n = 2 * n
    fars = [swap(both, "row", mask) for mask in (XA, XB, XAB)]
    weights.append(fetch(order, up_weight))
    x, g = join(
        order,
        (both, *fars),
        tuple((k, 0, n) for k in range(4)),
        tuple((k, n, n) for k in range(4)),
    )
    far_x, far_g = swap(x, "row", CORE), swap(g, "row", CORE)
    weights.append(fetch(order, down_weight))
    x = join(order, (x, far_x), ((0, 0, 4 * n), (1, 0, 4 * n))).reshape(8, n, -1)

    w_dims = (0, 0, 1)
    items = [(c, k) for c in range(CHUNKS) for k in range(3)]
    totals, fars = [None] * len(items), [None] * len(items)
    lefts = [x, x, None]

    def part(i, first, dtype):
        c, k = items[i]
        return partial_product(
            order, lefts[k], weights[k], w_dims[k], SUM_DIMS[i], first, chunks[c], dtype
        )

    grads = [None] * len(items)

    def send_step(i):
        k = items[i][1]
        if lefts[k] is None:
            lefts[k] = join(order, (g, far_g), ((0, 0, 4 * n), (1, 0, 4 * n))).reshape(x.shape)
        fars[i] = swap(part(i, 4, BF16), "col", COL[SUM_DIMS[i][0]])

    def keep_step(i):
        totals[i] = part(i, 0, F32)

    def halve_step(step, i):
        send, totals[i] = halve(order, totals[i], fars[i])
        fars[i] = swap(send, "col", COL[SUM_DIMS[i][step]])

    def swiglu_step(c):
        these = slice(3 * c, 3 * c + 3)
        hidden, gate_grad, up_grad = swiglu(order, totals[these], fars[these])
        grads[these] = gate_grad, up_grad, hidden
        for i in (3 * c, 3 * c + 1):
            fars[i] = swap(grads[i], "col", COL[GATHER_DIMS[i][0]])

    def grow(i, step):
        if step:
            n = fars[i].shape[0]
            grads[i] = join(order, (grads[i], fars[i]), ((0, 0, n), (1, 0, n)))
        if step < 3:
            fars[i] = swap(grads[i], "col", COL[GATHER_DIMS[i][step]])

    out = [None] * 3
    shapes = ((depth, width), (depth, width), (width, depth))

    def weight_step(*parts):
        kinds = [items[i][1] for i in parts]
        jobs = [(k, GATHER_DIMS[i][::-1], chunks[items[i][0]]) for i, k in zip(parts, kinds)]
        results = weight_grads(
            order,
            jobs,
            [lefts[k] for k in kinds],
            [grads[i] for i in parts],
            shapes,
            out,
        )
        for k, result in zip(sorted(set(kinds)), results):
            out[k] = result

    def input_step(c, first, before):
        these = slice(3 * c, 3 * c + 2)
        places = [dims[::-1] for dims in GATHER_DIMS[these]]
        return input_part(order, first, grads[these], places, weights[:2], chunks[c], before)

    send_step(0)
    send_step(1)
    send_step(2)
    send_step(3)
    send_step(4)
    keep_step(0)
    keep_step(1)
    keep_step(2)
    keep_step(3)
    send_step(5)
    halve_step(1, 0)
    halve_step(1, 1)
    halve_step(1, 2)
    halve_step(1, 3)
    keep_step(4)
    halve_step(1, 4)
    keep_step(5)
    halve_step(1, 5)
    halve_step(2, 0)
    halve_step(2, 1)
    halve_step(2, 2)
    halve_step(2, 3)
    halve_step(2, 4)
    halve_step(2, 5)
    swiglu_step(0)
    swiglu_step(1)
    grow(0, 1)
    grow(1, 1)
    both = beside(order, grads[2], grads[5])
    far = swap(both, "col", COL[GATHER_DIMS[2][0]])
    grow(3, 1)
    grow(4, 1)
    grow(0, 2)
    grow(1, 2)
    grow(3, 2)
    grow(4, 2)
    grads[2], grads[5] = split(order, both, far, CHUNKS)
    for i in (2, 5):
        fars[i] = swap(grads[i], "col", COL[GATHER_DIMS[i][1]])
    grow(0, 3)
    grow(1, 3)
    send, keep = input_step(0, 4, None), input_step(0, 0, None)
    grow(3, 3)
    grow(4, 3)
    send = input_step(1, 4, send)
    far = swap(send, "row", CORE)
    keep = input_step(1, 0, keep)

    n = x.shape[1]
    shape = (n, depth)
    own, *sends = order.run(
        small(
            core_kernel,
            [jax.ShapeDtypeStruct(shape, F32)] + [jax.ShapeDtypeStruct(shape, BF16)] * 3,
            2,
        ),
        keep,
        far,
    )
    rings = [swap(v, "row", mask) for v, mask in zip(sends, (XA, XB, XAB))]
    grow(2, 2)
    grow(5, 2)
    weight_step(0, 1)
    shape = jax.ShapeDtypeStruct((n // 2, depth), F32)
    keep, send = order.run(small(ring_kernel, [shape, shape], 4), own, *rings)
    far = swap(send, "row", ZHI)
    weight_step(3, 4)
    grow(2, 3)
    grow(5, 3)
    weight_step(2, 5)
    input_grad = (keep + far).astype(BF16)
    return (input_grad, *out)


def solution(mesh):
    return jax.shard_map(
        per_device,
        mesh=mesh,
        in_specs=(
            P("row", "col"),
            P("row", "col"),
            P("col", "row"),
            P("col", "row"),
            P("row", "col"),
        ),
        out_specs=(P("row", "col"), P("col", "row"), P("col", "row"), P("row", "col")),
        check_vma=False,
    )
```

```python
import functools

import jax
import jax.numpy as jnp
from jax import lax
from jax.experimental import pallas as pl
from jax.experimental.pallas import tpu as pltpu
from jax.sharding import PartitionSpec as P

BF16, F32 = jnp.bfloat16, jnp.float32
TILE = 256
CHUNKS = 2
VMEM = 20 * 1024 * 1024

COL = {"a": 2, "b": 6, "c": 1}
BIT = {"a": 4, "b": 2, "c": 1}
CORE, ZHI, XA, XB, XAB = 1, 2, 4, 12, 8

SUM_DIMS = ("abc", "bca", "cab", "abc", "bca", "cab")
GATHER_DIMS = ("bca", "cab", "cab", "bca", "acb", "cba")


def swap(value, axis, mask):
    size = lax.axis_size(axis)
    return lax.ppermute(value, axis, [(i, i ^ mask) for i in range(size)])

IN_VMEM = pl.BlockSpec(memory_space=pltpu.VMEM)
IN_SMEM = pl.BlockSpec(memory_space=pltpu.SMEM)
PARAMS = pltpu.CompilerParams(vmem_limit_bytes=VMEM)


SHORT = pl.CostEstimate(flops=1, bytes_accessed=1, transcendentals=0)


def block_at(place, mine, dims):
    name = sum(BIT[d] * ((place >> (2 - k)) & 1) for k, d in enumerate(dims))
    return name ^ mine


def place_of(block, mine, dims):
    bits = [(((block ^ mine) // BIT[d]) % 2) * (4 >> k) for k, d in enumerate(dims)]
    return bits[0] + bits[1] + bits[2]


class Order:
    def __init__(self, mine):
        self.mine = mine

    def run(self, call, *args):
        out = call(self.mine, *args)
        self.mine, out = lax.optimization_barrier((self.mine, out))
        return out


def small(kernel, shapes, count):
    return pl.pallas_call(
        lambda mine, *refs: kernel(*refs),
        out_shape=shapes,
        in_specs=[IN_SMEM] + [IN_VMEM] * count,
        out_specs=[IN_VMEM] * len(shapes),
        compiler_params=PARAMS,
        cost_estimate=SHORT,
    )


def join_kernel(plan, *refs):
    ins, outs = refs[: -len(plan)], refs[-len(plan) :]
    for out, pieces in zip(outs, plan):
        at = 0
        for which, start, size in pieces:
            out[at : at + size, :] = ins[which][start : start + size, :]
            at += size


def join(order, arrays, *plan):
    width = arrays[0].shape[1]
    shapes = [
        jax.ShapeDtypeStruct((sum(p[2] for p in pieces), width), arrays[0].dtype)
        for pieces in plan
    ]
    out = order.run(
        small(functools.partial(join_kernel, plan), shapes, len(arrays)), *arrays
    )
    return out if len(out) > 1 else out[0]


def fetch_kernel(mine_ref, w_ref, out_ref, sem):
    copy = pltpu.make_async_copy(w_ref, out_ref, sem)
    copy.start()
    copy.wait()


def fetch(order, weight):
    return order.run(
        pl.pallas_call(
            fetch_kernel,
            out_shape=jax.ShapeDtypeStruct(weight.shape, weight.dtype),
            in_specs=[IN_SMEM, pl.BlockSpec(memory_space=pltpu.HBM)],
            out_specs=IN_VMEM,
            scratch_shapes=[pltpu.SemaphoreType.DMA],
            compiler_params=PARAMS,
            cost_estimate=SHORT,
        ),
        weight,
    )


def part_kernel(w_dim, dims, first, cols, mine_ref, x_ref, w_ref, out_ref, x_scr):
    rows = x_ref.shape[1]
    for k in range(4):
        x_scr[k * rows : (k + 1) * rows, :] = x_ref[block_at(first + k, mine_ref[0], dims)]
    w = w_ref[:, cols] if w_dim == 0 else w_ref[cols, :]
    out_ref[...] = lax.dot_general(
        x_scr[...], w, (((1,), (w_dim,)), ((), ())), preferred_element_type=F32
    ).astype(out_ref.dtype)


def partial_product(order, blocks, weight, w_dim, dims, first, cols, dtype):
    _, rows, depth = blocks.shape
    width = cols.stop - cols.start
    call = pl.pallas_call(
        functools.partial(part_kernel, w_dim, dims, first, cols),
        out_shape=jax.ShapeDtypeStruct((4 * rows, width), dtype),
        in_specs=[IN_SMEM, IN_VMEM, IN_VMEM],
        out_specs=IN_VMEM,
        scratch_shapes=[pltpu.VMEM((4 * rows, depth), BF16)],
        compiler_params=PARAMS,
        cost_estimate=SHORT,
    )
    return order.run(call, blocks, weight)


def halve_kernel(keep_ref, far_ref, send_ref, total_ref):
    n = send_ref.shape[0]
    send_ref[...] = (keep_ref[n:, :] + far_ref[n:, :].astype(F32)).astype(BF16)
    total_ref[...] = keep_ref[:n, :] + far_ref[:n, :].astype(F32)


def halve(order, keep, far):
    shape = (far.shape[0] // 2, far.shape[1])
    shapes = [jax.ShapeDtypeStruct(shape, BF16), jax.ShapeDtypeStruct(shape, F32)]
    return order.run(small(halve_kernel, shapes, 2), keep, far)


def swiglu_kernel(*refs):
    gate, up, hidden_grad = (
        refs[2 * k][...] + refs[2 * k + 1][...].astype(F32) for k in range(3)
    )
    for ref, value in zip(refs[6:], swiglu_grads(gate, up, hidden_grad)):
        ref[...] = value


def swiglu(order, totals, fars):
    shape = jax.ShapeDtypeStruct(totals[0].shape, BF16)
    args = [a for pair in zip(totals, fars) for a in pair]
    return order.run(small(swiglu_kernel, [shape] * 3, 6), *args)


def beside_kernel(a_ref, b_ref, out_ref):
    width = a_ref.shape[1]
    out_ref[:, :width] = a_ref[...]
    out_ref[:, width:] = b_ref[...]


def beside(order, a, b):
    shape = jax.ShapeDtypeStruct((a.shape[0], a.shape[1] + b.shape[1]), a.dtype)
    return order.run(small(beside_kernel, [shape], 2), a, b)[0]


def split_kernel(near_ref, far_ref, *out_refs):
    rows, width = near_ref.shape[0], out_refs[0].shape[1]
    for k, ref in enumerate(out_refs):
        here = slice(k * width, (k + 1) * width)
        ref[:rows, :] = near_ref[:, here]
        ref[rows:, :] = far_ref[:, here]


def split(order, near, far, count):
    shape = jax.ShapeDtypeStruct((2 * near.shape[0], near.shape[1] // count), near.dtype)
    return order.run(small(split_kernel, [shape] * count, 2), near, far)


def reorder(dims, mine_ref, blocks_ref, out_ref):
    rows = blocks_ref.shape[1]
    for place in range(8):
        out_ref[place * rows : (place + 1) * rows, :] = blocks_ref[
            block_at(place, mine_ref[0], dims)
        ]


FIRST = (((0,), (0,)), ((), ()))
LAST = (((1,), (1,)), ((), ()))


def grads_kernel(jobs, mine_ref, *refs):
    count = len(jobs)
    lefts, grads = refs[:count], refs[count : 2 * count]
    kinds = sorted({kind for kind, _, _ in jobs})
    out_refs, (scrs, out_scrs, sems) = refs[-len(kinds) - 3 : -3], refs[-3:]
    copies = []
    for k, (kind, dims, cols) in enumerate(jobs):
        left_scr, out_scr, out_ref = scrs[k], out_scrs[k], out_refs[kinds.index(kind)]
        reorder(dims, mine_ref, lefts[k], left_scr)
        size = out_scr.shape[0]
        half = -(-size // 256) * 128
        for rows in (slice(0, half), slice(half, size)):
            if kind < 2:
                a, b = left_scr[:, rows], grads[k][...]
                there = out_ref.at[rows, cols]
            else:
                a, b = grads[k][:, rows], left_scr[...]
                there = out_ref.at[cols.start + rows.start : cols.start + rows.stop]
            out_scr[rows, :] = lax.dot_general(
                a, b, FIRST, preferred_element_type=F32
            ).astype(BF16)
            copies.append(pltpu.make_async_copy(out_scr.at[rows], there, sems.at[len(copies)]))
            copies[-1].start()
    for copy in copies:
        copy.wait()


def weight_grads(order, jobs, lefts, grads, shapes, befores):
    kinds = sorted({kind for kind, _, _ in jobs})
    in_hbm = pl.BlockSpec(memory_space=pltpu.HBM)
    known = [(at, befores[k]) for at, k in enumerate(kinds) if befores[k] is not None]
    sizes = [
        (shapes[kind][0], cols.stop - cols.start)
        if kind < 2
        else (cols.stop - cols.start, shapes[kind][1])
        for kind, _, cols in jobs
    ]
    flat = [(v.shape[0] * v.shape[1], v.shape[2]) for v in lefts]
    first = 1 + 2 * len(jobs)
    call = pl.pallas_call(
        functools.partial(grads_kernel, jobs),
        out_shape=[jax.ShapeDtypeStruct(shapes[k], BF16) for k in kinds],
        in_specs=[IN_SMEM] + [IN_VMEM] * (2 * len(jobs)) + [in_hbm] * len(known),
        out_specs=[pl.BlockSpec(memory_space=pl.ANY)] * len(kinds),
        scratch_shapes=[
            [pltpu.VMEM(shape, BF16) for shape in flat],
            [pltpu.VMEM(size, BF16) for size in sizes],
            pltpu.SemaphoreType.DMA((2 * len(jobs),)),
        ],
        input_output_aliases={first + at: k for at, (k, _) in enumerate(known)},
        compiler_params=PARAMS,
        cost_estimate=SHORT,
    )
    return order.run(call, *lefts, *grads, *(b for _, b in known))


def input_kernel(first, gate_dims, up_dims, cols, mine_ref, gg_ref, ug_ref, wg_ref, wu_ref, *rest):
    out_ref, gg_scr, ug_scr = rest[-3:]
    mine = mine_ref[0]
    rows = gg_ref.shape[1]
    for k in range(4):
        here = slice(k * rows, (k + 1) * rows)
        gg_scr[here, :] = gg_ref[place_of(first + k, mine, gate_dims)]
        ug_scr[here, :] = ug_ref[place_of(first + k, mine, up_dims)]
    for i in range(0, out_ref.shape[1], TILE):
        here = slice(i, i + TILE)
        part = lax.dot_general(
            gg_scr[...], wg_ref[here, cols], LAST, preferred_element_type=F32
        ) + lax.dot_general(ug_scr[...], wu_ref[here, cols], LAST, preferred_element_type=F32)
        out_ref[:, here] = part + rest[0][:, here] if len(rest) == 4 else part


def input_part(order, first, grads, dims, weights, cols, before):
    tokens, width = grads[0].shape
    depth = weights[0].shape[0]
    half = pltpu.VMEM((tokens // 2, width), BF16)
    blocked = (8, tokens // 8, width)
    more = [] if before is None else [before]
    call = pl.pallas_call(
        functools.partial(input_kernel, first, *dims, cols),
        out_shape=jax.ShapeDtypeStruct((tokens // 2, depth), F32),
        in_specs=[IN_SMEM] + [IN_VMEM] * (4 + len(more)),
        out_specs=IN_VMEM,
        scratch_shapes=[half, half],
        compiler_params=PARAMS,
        cost_estimate=SHORT,
    )
    return order.run(call, *(v.reshape(blocked) for v in grads), *weights, *more)


def core_kernel(keep_ref, far_ref, own_ref, *send_refs):
    n = own_ref.shape[0]
    own_ref[...] = keep_ref[:n, :] + far_ref[:n, :]
    for k, ref in enumerate(send_refs, 1):
        here = slice(k * n, (k + 1) * n)
        ref[...] = (keep_ref[here, :] + far_ref[here, :]).astype(BF16)


def ring_kernel(own_ref, a_ref, b_ref, c_ref, keep_ref, send_ref):
    total = (own_ref[...] + a_ref[...].astype(F32)) + (
        b_ref[...].astype(F32) + c_ref[...].astype(F32)
    )
    n = keep_ref.shape[0]
    keep_ref[...] = total[:n]
    send_ref[...] = total[n:]


def swiglu_grads(gate, up, hidden_grad):
    sig = jax.nn.sigmoid(gate)
    hidden = (gate * sig * up).astype(BF16)
    gate_grad = (hidden_grad * up * sig * (1.0 + gate * (1.0 - sig))).astype(BF16)
    up_grad = (hidden_grad * gate * sig).astype(BF16)
    return hidden, gate_grad, up_grad


def per_device(inputs, out_grad, gate_weight, up_weight, down_weight):
    col = lax.axis_index("col")
    y_high, y_low = (col >> 2) & 1, (col >> 1) & 1
    mine = (y_high ^ y_low) * BIT["a"] + y_high * BIT["b"] + (col & 1) * BIT["c"]
    mine = mine.astype(jnp.int32).reshape(1)

    order = Order(mine)
    depth, width = gate_weight.shape
    size = width // CHUNKS
    chunks = [slice(k * size, (k + 1) * size) for k in range(CHUNKS)]
    n = inputs.shape[0]
    far_x, far_g = swap(inputs, "row", ZHI), swap(out_grad, "row", ZHI)
    weights = [fetch(order, gate_weight)]
    both = join(order, (inputs, far_x, out_grad, far_g), tuple((k, 0, n) for k in range(4)))
    n = 2 * n
    fars = [swap(both, "row", mask) for mask in (XA, XB, XAB)]
    weights.append(fetch(order, up_weight))
    x, g = join(
        order,
        (both, *fars),
        tuple((k, 0, n) for k in range(4)),
        tuple((k, n, n) for k in range(4)),
    )
    far_x, far_g = swap(x, "row", CORE), swap(g, "row", CORE)
    weights.append(fetch(order, down_weight))
    x = join(order, (x, far_x), ((0, 0, 4 * n), (1, 0, 4 * n))).reshape(8, n, -1)

    w_dims = (0, 0, 1)
    items = [(c, k) for c in range(CHUNKS) for k in range(3)]
    totals, fars = [None] * len(items), [None] * len(items)
    lefts = [x, x, None]

    def part(i, first, dtype):
        c, k = items[i]
        return partial_product(
            order, lefts[k], weights[k], w_dims[k], SUM_DIMS[i], first, chunks[c], dtype
        )

    grads = [None] * len(items)

    def send_step(i):
        k = items[i][1]
        if lefts[k] is None:
            lefts[k] = join(order, (g, far_g), ((0, 0, 4 * n), (1, 0, 4 * n))).reshape(x.shape)
        fars[i] = swap(part(i, 4, BF16), "col", COL[SUM_DIMS[i][0]])

    def keep_step(i):
        totals[i] = part(i, 0, F32)

    def halve_step(step, i):
        send, totals[i] = halve(order, totals[i], fars[i])
        fars[i] = swap(send, "col", COL[SUM_DIMS[i][step]])

    def swiglu_step(c):
        these = slice(3 * c, 3 * c + 3)
        hidden, gate_grad, up_grad = swiglu(order, totals[these], fars[these])
        grads[these] = gate_grad, up_grad, hidden
        for i in (3 * c, 3 * c + 1):
            fars[i] = swap(grads[i], "col", COL[GATHER_DIMS[i][0]])

    def grow(i, step):
        if step:
            n = fars[i].shape[0]
            grads[i] = join(order, (grads[i], fars[i]), ((0, 0, n), (1, 0, n)))
        if step < 3:
            fars[i] = swap(grads[i], "col", COL[GATHER_DIMS[i][step]])

    out = [None] * 3
    shapes = ((depth, width), (depth, width), (width, depth))

    def weight_step(*parts):
        kinds = [items[i][1] for i in parts]
        jobs = [(k, GATHER_DIMS[i][::-1], chunks[items[i][0]]) for i, k in zip(parts, kinds)]
        results = weight_grads(
            order,
            jobs,
            [lefts[k] for k in kinds],
            [grads[i] for i in parts],
            shapes,
            out,
        )
        for k, result in zip(sorted(set(kinds)), results):
            out[k] = result

    def input_step(c, first, before):
        these = slice(3 * c, 3 * c + 2)
        places = [dims[::-1] for dims in GATHER_DIMS[these]]
        return input_part(order, first, grads[these], places, weights[:2], chunks[c], before)

    send_step(0)
    send_step(1)
    send_step(2)
    send_step(3)
    send_step(4)
    keep_step(0)
    keep_step(1)
    keep_step(2)
    keep_step(3)
    send_step(5)
    halve_step(1, 0)
    halve_step(1, 1)
    keep_step(4)
    halve_step(1, 2)
    keep_step(5)
    halve_step(1, 3)
    halve_step(1, 4)
    halve_step(1, 5)
    halve_step(2, 0)
    halve_step(2, 1)
    halve_step(2, 2)
    halve_step(2, 3)
    halve_step(2, 4)
    halve_step(2, 5)
    swiglu_step(0)
    swiglu_step(1)
    grow(0, 1)
    grow(1, 1)
    grow(3, 1)
    grow(4, 1)
    both = beside(order, grads[2], grads[5])
    far = swap(both, "col", COL[GATHER_DIMS[2][0]])
    grow(0, 2)
    grow(1, 2)
    grow(3, 2)
    grow(4, 2)
    grow(0, 3)
    grow(1, 3)
    send, keep = input_step(0, 4, None), input_step(0, 0, None)
    grads[2], grads[5] = split(order, both, far, CHUNKS)
    for i in (2, 5):
        fars[i] = swap(grads[i], "col", COL[GATHER_DIMS[i][1]])
    grow(3, 3)
    grow(4, 3)
    send = input_step(1, 4, send)
    far = swap(send, "row", CORE)
    keep = input_step(1, 0, keep)

    n = x.shape[1]
    shape = (n, depth)
    own, *sends = order.run(
        small(
            core_kernel,
            [jax.ShapeDtypeStruct(shape, F32)] + [jax.ShapeDtypeStruct(shape, BF16)] * 3,
            2,
        ),
        keep,
        far,
    )
    rings = [swap(v, "row", mask) for v, mask in zip(sends, (XA, XB, XAB))]
    grow(2, 2)
    grow(5, 2)
    weight_step(0, 1)
    shape = jax.ShapeDtypeStruct((n // 2, depth), F32)
    keep, send = order.run(small(ring_kernel, [shape, shape], 4), own, *rings)
    far = swap(send, "row", ZHI)
    weight_step(3, 4)
    grow(2, 3)
    grow(5, 3)
    weight_step(2, 5)
    input_grad = (keep + far).astype(BF16)
    return (input_grad, *out)


def solution(mesh):
    return jax.shard_map(
        per_device,
        mesh=mesh,
        in_specs=(
            P("row", "col"),
            P("row", "col"),
            P("col", "row"),
            P("col", "row"),
            P("row", "col"),
        ),
        out_specs=(P("row", "col"), P("col", "row"), P("col", "row"), P("row", "col")),
        check_vma=False,
    )
```

```python
import functools

import jax
import jax.numpy as jnp
from jax import lax
from jax.experimental import pallas as pl
from jax.experimental.pallas import tpu as pltpu
from jax.sharding import PartitionSpec as P

BF16, F32 = jnp.bfloat16, jnp.float32
TILE = 256
CHUNKS = 2
VMEM = 20 * 1024 * 1024

COL = {"a": 2, "b": 6, "c": 1}
BIT = {"a": 4, "b": 2, "c": 1}
CORE, ZHI, XA, XB, XAB = 1, 2, 4, 12, 8

SUM_DIMS = ("abc", "bca", "cab", "abc", "bca", "cab")
GATHER_DIMS = ("bca", "cab", "cab", "bca", "acb", "cba")


def swap(value, axis, mask):
    size = lax.axis_size(axis)
    return lax.ppermute(value, axis, [(i, i ^ mask) for i in range(size)])

IN_VMEM = pl.BlockSpec(memory_space=pltpu.VMEM)
IN_SMEM = pl.BlockSpec(memory_space=pltpu.SMEM)
PARAMS = pltpu.CompilerParams(vmem_limit_bytes=VMEM)


SHORT = pl.CostEstimate(flops=1, bytes_accessed=1, transcendentals=0)


def block_at(place, mine, dims):
    name = sum(BIT[d] * ((place >> (2 - k)) & 1) for k, d in enumerate(dims))
    return name ^ mine


def place_of(block, mine, dims):
    bits = [(((block ^ mine) // BIT[d]) % 2) * (4 >> k) for k, d in enumerate(dims)]
    return bits[0] + bits[1] + bits[2]


class Order:
    def __init__(self, mine):
        self.mine = mine

    def run(self, call, *args):
        out = call(self.mine, *args)
        self.mine, out = lax.optimization_barrier((self.mine, out))
        return out


def small(kernel, shapes, count):
    return pl.pallas_call(
        lambda mine, *refs: kernel(*refs),
        out_shape=shapes,
        in_specs=[IN_SMEM] + [IN_VMEM] * count,
        out_specs=[IN_VMEM] * len(shapes),
        compiler_params=PARAMS,
        cost_estimate=SHORT,
    )


def join_kernel(plan, *refs):
    ins, outs = refs[: -len(plan)], refs[-len(plan) :]
    for out, pieces in zip(outs, plan):
        at = 0
        for which, start, size in pieces:
            out[at : at + size, :] = ins[which][start : start + size, :]
            at += size


def join(order, arrays, *plan):
    width = arrays[0].shape[1]
    shapes = [
        jax.ShapeDtypeStruct((sum(p[2] for p in pieces), width), arrays[0].dtype)
        for pieces in plan
    ]
    out = order.run(
        small(functools.partial(join_kernel, plan), shapes, len(arrays)), *arrays
    )
    return out if len(out) > 1 else out[0]


def fetch_kernel(mine_ref, w_ref, out_ref, sem):
    copy = pltpu.make_async_copy(w_ref, out_ref, sem)
    copy.start()
    copy.wait()


def fetch(order, weight):
    return order.run(
        pl.pallas_call(
            fetch_kernel,
            out_shape=jax.ShapeDtypeStruct(weight.shape, weight.dtype),
            in_specs=[IN_SMEM, pl.BlockSpec(memory_space=pltpu.HBM)],
            out_specs=IN_VMEM,
            scratch_shapes=[pltpu.SemaphoreType.DMA],
            compiler_params=PARAMS,
            cost_estimate=SHORT,
        ),
        weight,
    )


def part_kernel(w_dim, dims, first, cols, mine_ref, x_ref, w_ref, out_ref, x_scr):
    rows = x_ref.shape[1]
    for k in range(4):
        x_scr[k * rows : (k + 1) * rows, :] = x_ref[block_at(first + k, mine_ref[0], dims)]
    w = w_ref[:, cols] if w_dim == 0 else w_ref[cols, :]
    out_ref[...] = lax.dot_general(
        x_scr[...], w, (((1,), (w_dim,)), ((), ())), preferred_element_type=F32
    ).astype(out_ref.dtype)


def partial_product(order, blocks, weight, w_dim, dims, first, cols, dtype):
    _, rows, depth = blocks.shape
    width = cols.stop - cols.start
    call = pl.pallas_call(
        functools.partial(part_kernel, w_dim, dims, first, cols),
        out_shape=jax.ShapeDtypeStruct((4 * rows, width), dtype),
        in_specs=[IN_SMEM, IN_VMEM, IN_VMEM],
        out_specs=IN_VMEM,
        scratch_shapes=[pltpu.VMEM((4 * rows, depth), BF16)],
        compiler_params=PARAMS,
        cost_estimate=SHORT,
    )
    return order.run(call, blocks, weight)


def halve_kernel(keep_ref, far_ref, send_ref, total_ref):
    n = send_ref.shape[0]
    send_ref[...] = (keep_ref[n:, :] + far_ref[n:, :].astype(F32)).astype(BF16)
    total_ref[...] = keep_ref[:n, :] + far_ref[:n, :].astype(F32)


def halve(order, keep, far):
    shape = (far.shape[0] // 2, far.shape[1])
    shapes = [jax.ShapeDtypeStruct(shape, BF16), jax.ShapeDtypeStruct(shape, F32)]
    return order.run(small(halve_kernel, shapes, 2), keep, far)


def swiglu_kernel(*refs):
    gate, up, hidden_grad = (
        refs[2 * k][...] + refs[2 * k + 1][...].astype(F32) for k in range(3)
    )
    for ref, value in zip(refs[6:], swiglu_grads(gate, up, hidden_grad)):
        ref[...] = value


def swiglu(order, totals, fars):
    shape = jax.ShapeDtypeStruct(totals[0].shape, BF16)
    args = [a for pair in zip(totals, fars) for a in pair]
    return order.run(small(swiglu_kernel, [shape] * 3, 6), *args)


def beside_kernel(a_ref, b_ref, out_ref):
    width = a_ref.shape[1]
    out_ref[:, :width] = a_ref[...]
    out_ref[:, width:] = b_ref[...]


def beside(order, a, b):
    shape = jax.ShapeDtypeStruct((a.shape[0], a.shape[1] + b.shape[1]), a.dtype)
    return order.run(small(beside_kernel, [shape], 2), a, b)[0]


def split_kernel(near_ref, far_ref, *out_refs):
    rows, width = near_ref.shape[0], out_refs[0].shape[1]
    for k, ref in enumerate(out_refs):
        here = slice(k * width, (k + 1) * width)
        ref[:rows, :] = near_ref[:, here]
        ref[rows:, :] = far_ref[:, here]


def split(order, near, far, count):
    shape = jax.ShapeDtypeStruct((2 * near.shape[0], near.shape[1] // count), near.dtype)
    return order.run(small(split_kernel, [shape] * count, 2), near, far)


def reorder(dims, mine_ref, blocks_ref, out_ref):
    rows = blocks_ref.shape[1]
    for place in range(8):
        out_ref[place * rows : (place + 1) * rows, :] = blocks_ref[
            block_at(place, mine_ref[0], dims)
        ]


FIRST = (((0,), (0,)), ((), ()))
LAST = (((1,), (1,)), ((), ()))


def grads_kernel(jobs, mine_ref, *refs):
    count = len(jobs)
    lefts, grads = refs[:count], refs[count : 2 * count]
    kinds = sorted({kind for kind, _, _ in jobs})
    out_refs, (scrs, out_scrs, sems) = refs[-len(kinds) - 3 : -3], refs[-3:]
    copies = []
    for k, (kind, dims, cols) in enumerate(jobs):
        left_scr, out_scr, out_ref = scrs[k], out_scrs[k], out_refs[kinds.index(kind)]
        reorder(dims, mine_ref, lefts[k], left_scr)
        size = out_scr.shape[0]
        half = -(-size // 256) * 128
        for rows in (slice(0, half), slice(half, size)):
            if kind < 2:
                a, b = left_scr[:, rows], grads[k][...]
                there = out_ref.at[rows, cols]
            else:
                a, b = grads[k][:, rows], left_scr[...]
                there = out_ref.at[cols.start + rows.start : cols.start + rows.stop]
            out_scr[rows, :] = lax.dot_general(
                a, b, FIRST, preferred_element_type=F32
            ).astype(BF16)
            copies.append(pltpu.make_async_copy(out_scr.at[rows], there, sems.at[len(copies)]))
            copies[-1].start()
    for copy in copies:
        copy.wait()


def weight_grads(order, jobs, lefts, grads, shapes, befores):
    kinds = sorted({kind for kind, _, _ in jobs})
    in_hbm = pl.BlockSpec(memory_space=pltpu.HBM)
    known = [(at, befores[k]) for at, k in enumerate(kinds) if befores[k] is not None]
    sizes = [
        (shapes[kind][0], cols.stop - cols.start)
        if kind < 2
        else (cols.stop - cols.start, shapes[kind][1])
        for kind, _, cols in jobs
    ]
    flat = [(v.shape[0] * v.shape[1], v.shape[2]) for v in lefts]
    first = 1 + 2 * len(jobs)
    call = pl.pallas_call(
        functools.partial(grads_kernel, jobs),
        out_shape=[jax.ShapeDtypeStruct(shapes[k], BF16) for k in kinds],
        in_specs=[IN_SMEM] + [IN_VMEM] * (2 * len(jobs)) + [in_hbm] * len(known),
        out_specs=[pl.BlockSpec(memory_space=pl.ANY)] * len(kinds),
        scratch_shapes=[
            [pltpu.VMEM(shape, BF16) for shape in flat],
            [pltpu.VMEM(size, BF16) for size in sizes],
            pltpu.SemaphoreType.DMA((2 * len(jobs),)),
        ],
        input_output_aliases={first + at: k for at, (k, _) in enumerate(known)},
        compiler_params=PARAMS,
        cost_estimate=SHORT,
    )
    return order.run(call, *lefts, *grads, *(b for _, b in known))


def input_kernel(first, gate_dims, up_dims, cols, mine_ref, gg_ref, ug_ref, wg_ref, wu_ref, *rest):
    out_ref, gg_scr, ug_scr = rest[-3:]
    mine = mine_ref[0]
    rows = gg_ref.shape[1]
    for k in range(4):
        here = slice(k * rows, (k + 1) * rows)
        gg_scr[here, :] = gg_ref[place_of(first + k, mine, gate_dims)]
        ug_scr[here, :] = ug_ref[place_of(first + k, mine, up_dims)]
    for i in range(0, out_ref.shape[1], TILE):
        here = slice(i, i + TILE)
        part = lax.dot_general(
            gg_scr[...], wg_ref[here, cols], LAST, preferred_element_type=F32
        ) + lax.dot_general(ug_scr[...], wu_ref[here, cols], LAST, preferred_element_type=F32)
        out_ref[:, here] = part + rest[0][:, here] if len(rest) == 4 else part


def input_part(order, first, grads, dims, weights, cols, before):
    tokens, width = grads[0].shape
    depth = weights[0].shape[0]
    half = pltpu.VMEM((tokens // 2, width), BF16)
    blocked = (8, tokens // 8, width)
    more = [] if before is None else [before]
    call = pl.pallas_call(
        functools.partial(input_kernel, first, *dims, cols),
        out_shape=jax.ShapeDtypeStruct((tokens // 2, depth), F32),
        in_specs=[IN_SMEM] + [IN_VMEM] * (4 + len(more)),
        out_specs=IN_VMEM,
        scratch_shapes=[half, half],
        compiler_params=PARAMS,
        cost_estimate=SHORT,
    )
    return order.run(call, *(v.reshape(blocked) for v in grads), *weights, *more)


def core_kernel(keep_ref, far_ref, own_ref, *send_refs):
    n = own_ref.shape[0]
    own_ref[...] = keep_ref[:n, :] + far_ref[:n, :]
    for k, ref in enumerate(send_refs, 1):
        here = slice(k * n, (k + 1) * n)
        ref[...] = (keep_ref[here, :] + far_ref[here, :]).astype(BF16)


def ring_kernel(own_ref, a_ref, b_ref, c_ref, keep_ref, send_ref):
    total = (own_ref[...] + a_ref[...].astype(F32)) + (
        b_ref[...].astype(F32) + c_ref[...].astype(F32)
    )
    n = keep_ref.shape[0]
    keep_ref[...] = total[:n]
    send_ref[...] = total[n:]


def swiglu_grads(gate, up, hidden_grad):
    sig = jax.nn.sigmoid(gate)
    hidden = (gate * sig * up).astype(BF16)
    gate_grad = (hidden_grad * up * sig * (1.0 + gate * (1.0 - sig))).astype(BF16)
    up_grad = (hidden_grad * gate * sig).astype(BF16)
    return hidden, gate_grad, up_grad


def per_device(inputs, out_grad, gate_weight, up_weight, down_weight):
    col = lax.axis_index("col")
    y_high, y_low = (col >> 2) & 1, (col >> 1) & 1
    mine = (y_high ^ y_low) * BIT["a"] + y_high * BIT["b"] + (col & 1) * BIT["c"]
    mine = mine.astype(jnp.int32).reshape(1)

    order = Order(mine)
    depth, width = gate_weight.shape
    size = width // CHUNKS
    chunks = [slice(k * size, (k + 1) * size) for k in range(CHUNKS)]
    n = inputs.shape[0]
    far_x, far_g = swap(inputs, "row", ZHI), swap(out_grad, "row", ZHI)
    weights = [fetch(order, gate_weight)]
    both = join(order, (inputs, far_x, out_grad, far_g), tuple((k, 0, n) for k in range(4)))
    n = 2 * n
    far = swap(both, "row", XAB)
    fars = [swap(both, "row", mask) for mask in (XA, XB)] + [far]
    weights.append(fetch(order, up_weight))
    x, g = join(
        order,
        (both, *fars),
        tuple((k, 0, n) for k in range(4)),
        tuple((k, n, n) for k in range(4)),
    )
    far_x, far_g = swap(x, "row", CORE), swap(g, "row", CORE)
    weights.append(fetch(order, down_weight))
    x = join(order, (x, far_x), ((0, 0, 4 * n), (1, 0, 4 * n))).reshape(8, n, -1)

    w_dims = (0, 0, 1)
    items = [(c, k) for c in range(CHUNKS) for k in range(3)]
    totals, fars = [None] * len(items), [None] * len(items)
    lefts = [x, x, None]

    def part(i, first, dtype):
        c, k = items[i]
        return partial_product(
            order, lefts[k], weights[k], w_dims[k], SUM_DIMS[i], first, chunks[c], dtype
        )

    grads = [None] * len(items)

    def send_step(i):
        k = items[i][1]
        if lefts[k] is None:
            lefts[k] = join(order, (g, far_g), ((0, 0, 4 * n), (1, 0, 4 * n))).reshape(x.shape)
        fars[i] = swap(part(i, 4, BF16), "col", COL[SUM_DIMS[i][0]])

    def keep_step(i):
        totals[i] = part(i, 0, F32)

    def halve_step(step, i):
        send, totals[i] = halve(order, totals[i], fars[i])
        fars[i] = swap(send, "col", COL[SUM_DIMS[i][step]])

    def swiglu_step(c):
        these = slice(3 * c, 3 * c + 3)
        hidden, gate_grad, up_grad = swiglu(order, totals[these], fars[these])
        grads[these] = gate_grad, up_grad, hidden
        for i in (3 * c, 3 * c + 1):
            fars[i] = swap(grads[i], "col", COL[GATHER_DIMS[i][0]])

    def grow(i, step):
        if step:
            n = fars[i].shape[0]
            grads[i] = join(order, (grads[i], fars[i]), ((0, 0, n), (1, 0, n)))
        if step < 3:
            fars[i] = swap(grads[i], "col", COL[GATHER_DIMS[i][step]])

    out = [None] * 3
    shapes = ((depth, width), (depth, width), (width, depth))

    def weight_step(*parts):
        kinds = [items[i][1] for i in parts]
        jobs = [(k, GATHER_DIMS[i][::-1], chunks[items[i][0]]) for i, k in zip(parts, kinds)]
        results = weight_grads(
            order,
            jobs,
            [lefts[k] for k in kinds],
            [grads[i] for i in parts],
            shapes,
            out,
        )
        for k, result in zip(sorted(set(kinds)), results):
            out[k] = result

    def input_step(c, first, before):
        these = slice(3 * c, 3 * c + 2)
        places = [dims[::-1] for dims in GATHER_DIMS[these]]
        return input_part(order, first, grads[these], places, weights[:2], chunks[c], before)

    send_step(0)
    send_step(1)
    send_step(2)
    send_step(3)
    send_step(4)
    keep_step(0)
    keep_step(1)
    keep_step(2)
    keep_step(3)
    send_step(5)
    halve_step(1, 0)
    halve_step(1, 1)
    keep_step(4)
    halve_step(1, 2)
    keep_step(5)
    halve_step(1, 3)
    halve_step(1, 4)
    halve_step(1, 5)
    halve_step(2, 0)
    halve_step(2, 1)
    halve_step(2, 2)
    halve_step(2, 3)
    halve_step(2, 4)
    halve_step(2, 5)
    swiglu_step(0)
    swiglu_step(1)
    grow(0, 1)
    grow(1, 1)
    grow(3, 1)
    grow(4, 1)
    both = beside(order, grads[2], grads[5])
    far = swap(both, "col", COL[GATHER_DIMS[2][0]])
    grow(0, 2)
    grow(1, 2)
    grow(3, 2)
    grow(4, 2)
    grow(0, 3)
    grow(1, 3)
    send, keep = input_step(0, 4, None), input_step(0, 0, None)
    grads[2], grads[5] = split(order, both, far, CHUNKS)
    for i in (2, 5):
        fars[i] = swap(grads[i], "col", COL[GATHER_DIMS[i][1]])
    grow(3, 3)
    grow(4, 3)
    send = input_step(1, 4, send)
    far = swap(send, "row", CORE)
    keep = input_step(1, 0, keep)

    n = x.shape[1]
    shape = (n, depth)
    own, *sends = order.run(
        small(
            core_kernel,
            [jax.ShapeDtypeStruct(shape, F32)] + [jax.ShapeDtypeStruct(shape, BF16)] * 3,
            2,
        ),
        keep,
        far,
    )
    ring = swap(sends[2], "row", XAB)
    rings = [swap(v, "row", mask) for v, mask in zip(sends, (XA, XB))] + [ring]
    grow(2, 2)
    grow(5, 2)
    weight_step(0, 1)
    shape = jax.ShapeDtypeStruct((n // 2, depth), F32)
    keep, send = order.run(small(ring_kernel, [shape, shape], 4), own, *rings)
    far = swap(send, "row", ZHI)
    weight_step(3, 4)
    grow(2, 3)
    grow(5, 3)
    weight_step(2, 5)
    input_grad = (keep + far).astype(BF16)
    return (input_grad, *out)


def solution(mesh):
    return jax.shard_map(
        per_device,
        mesh=mesh,
        in_specs=(
            P("row", "col"),
            P("row", "col"),
            P("col", "row"),
            P("col", "row"),
            P("row", "col"),
        ),
        out_specs=(P("row", "col"), P("col", "row"), P("col", "row"), P("row", "col")),
        check_vma=False,
    )
```
